32 devices in a mesh: row: 4 (over x, core), col: 8 (over z, y).
Axes of the slice: x: 2, y: 2, z: 4, core: 2. Of those that a mesh axis runs over, the one named last changes fastest.
Arguments:
- sdf_grids: bfloat16 [16384, 4096], P(('row', 'col')), may hold values from -6 to 6
- grain_poses: float32 [12, 16384], P(None, ('row', 'col')), may hold values from -4 to 4
- surface_nodes: float32 [16384, 768], P(('row', 'col')), may hold values from -5 to 5
- send_list: int32 [4, 8, 8, 32], P('row', 'col'), may hold values from 0 to 511, as said below
- pair_first: int32 [4096], P(('row', 'col')), may hold values from 0 to 511
- pair_sdf: int32 [4096], P(('row', 'col')), may hold values from 0 to 767, as said below
- pair_pose: int32 [4096], P(('row', 'col')), may hold values from 0 to 4607, as said below
- pair_live: int32 [4096], P(('row', 'col')), may hold values from 0 to 1, as said below
- knot_cells: int32 [4096, 768], P(('row', 'col')), may hold values from 1 to 13
- offsets: float32 [4096, 768], P(('row', 'col')), may hold values from 0 to 1
Outputs:
- grain_loads: float32 [6, 16384], P(None, ('row', 'col'))
The draws below stay inside these ranges and needn't reach their ends.
Inputs may be any that keep to these rules, and one draw needn't show every extreme that they name: `send_list`: the 8 lists of one device name distinct own grains each; list d is meant for the neighbour at offset d of the direction order; the neighbour's pairs name only slots of list d below a count from 8 to 32; on every device one of its 8 lists has count 32. `pair_sdf`: below 512: an own grain other than the first grain. From 512 on: ghost block d and slot s of an existing neighbour. `pair_pose`: names the pose of the same grain as pair_sdf: an own grain in the centre block, or the neighbour's listed grain. `pair_live`: on each device the live slots come first; their number is 128 divided by 1, 2 or 4, and some device has all slots live.
All inputs are finite; a program needn't handle non-finite values.
Results may differ from the reference program's by a relative error of at most 0.0057.
Values may be sent and summed in bfloat16 or wider, within the bound.
A program may use at most 64 MiB of HBM per device.

```python
import jax
import jax.numpy as jnp
from jax import lax

GRID = 16
NODES = 256
GR_DEV = 512
GHOST = 32
PAIRS_DEV = 128
GRAINS = 16384
PAIRS = 4096
N_ROW = 4
N_COL = 8


DIRECTIONS = ((-1, -1), (-1, 0), (-1, 1), (0, -1), (0, 1), (1, -1), (1, 0), (1, 1))


def layout(key):
    devices = N_ROW * N_COL
    key_list = jax.random.split(jax.random.fold_in(key, 101), devices * 8)
    listed = jax.vmap(lambda single: jax.random.permutation(single, GR_DEV)[:GHOST])(key_list)
    listed = listed.astype(jnp.int32).reshape(N_ROW, N_COL, 8, GHOST)
    counts = jax.random.randint(jax.random.fold_in(key, 102), (N_ROW, N_COL, 8), max(1, GHOST // 4), GHOST + 1)
    full_dir = jax.random.randint(jax.random.fold_in(key, 103), (N_ROW, N_COL, 1), 0, 8)
    counts = jnp.where(jnp.arange(8, dtype=jnp.int32)[None, None, :] == full_dir, GHOST, counts)
    grid_shape = (N_ROW, N_COL, PAIRS_DEV)
    owner_grain = jax.random.randint(jax.random.fold_in(key, 104), grid_shape, 0, GR_DEV)
    partner = (owner_grain + 1 + jax.random.randint(jax.random.fold_in(key, 105), grid_shape, 0, GR_DEV - 1)) % GR_DEV
    wanted = jax.random.randint(jax.random.fold_in(key, 106), grid_shape, 0, 2)
    direction = jax.random.randint(jax.random.fold_in(key, 107), grid_shape, 0, 8)
    raw_slot = jax.random.randint(jax.random.fold_in(key, 108), grid_shape, 0, GHOST)
    step_table = jnp.array(DIRECTIONS, dtype=jnp.int32)
    row_at = jnp.arange(N_ROW, dtype=jnp.int32)[:, None, None] + step_table[direction, 0]
    col_at = jnp.arange(N_COL, dtype=jnp.int32)[None, :, None] + step_table[direction, 1]
    inside = (row_at >= 0) & (row_at < N_ROW) & (col_at >= 0) & (col_at < N_COL)
    row_at = jnp.clip(row_at, 0, N_ROW - 1)
    col_at = jnp.clip(col_at, 0, N_COL - 1)
    reverse = 7 - direction
    available = counts[row_at, col_at, reverse]
    slot_pick = raw_slot % available
    grain_id = listed[row_at, col_at, reverse, slot_pick]
    is_ghost = (wanted == 1) & inside
    halo_block = jnp.where(direction < 4, direction, direction + 1)
    sdf_rows = jnp.where(is_ghost, GR_DEV + direction * GHOST + slot_pick, partner)
    pose_rows = jnp.where(is_ghost, halo_block * GR_DEV + grain_id, 4 * GR_DEV + partner)
    return (listed, owner_grain.reshape(-1), sdf_rows.reshape(-1), pose_rows.reshape(-1))


def draw_send_list(key, part):
    return layout(key)[0].astype(jnp.int32)


def draw_pair_first(key, part):
    return layout(key)[1].astype(jnp.int32)


def draw_pair_sdf(key, part):
    return layout(key)[2].astype(jnp.int32)


def draw_pair_pose(key, part):
    return layout(key)[3].astype(jnp.int32)


def draw_pair_live(key, part):
    devices = N_ROW * N_COL
    halving = jax.random.randint(jax.random.fold_in(key, 201), (devices,), 0, 3)
    live_count = jnp.right_shift(jnp.full((devices,), PAIRS_DEV, jnp.int32), halving)
    busiest = jax.random.randint(jax.random.fold_in(key, 202), (1,), 0, devices)
    live_count = jnp.where(jnp.arange(devices, dtype=jnp.int32) == busiest, PAIRS_DEV, live_count)
    live = jnp.arange(PAIRS_DEV, dtype=jnp.int32)[None, :] < live_count[:, None]
    return live.astype(jnp.int32).reshape(-1)


def set_ends(result, own_key, smallest, largest):
    extent = result.shape
    place = [jax.random.randint(jax.random.fold_in(own_key, axis), (), 0, extent[axis]) for axis in range(len(extent))]
    result = result.at[tuple(place)].set(smallest)
    longest = extent.index(max(extent))
    place[longest] = (place[longest] + 1) % extent[longest]
    return result.at[tuple(place)].set(largest)


def steps_of(rng, shape, cuts, low, top_value):
    level = 1.0
    for dim, shards_of in cuts:
        draws = jax.random.uniform(jax.random.fold_in(jax.random.fold_in(rng, 6), dim), (shards_of,), jnp.float32, low / len(cuts), top_value / len(cuts))
        level = level * jnp.repeat(jnp.exp(draws), shape[dim] // shards_of).reshape((-1,) + (1,) * (len(shape) - 1 - dim))
    return level


def bell_draw(key, dims, spread, reach, cuts=(), held_as=jnp.bfloat16):
    values = spread * jax.random.normal(key, dims, jnp.float32)
    if cuts:
        values = values * steps_of(key, dims, cuts, -0.22, 0.18)
    return jnp.clip(values, -reach, reach).astype(held_as)


def setup_inputs(seed: int = 0) -> dict:
    keys = jax.random.split(jax.random.key(seed), 11)
    sdf_grids = bell_draw(keys[0], (GRAINS, GRID * GRID * GRID), 1.0, 6.0, ((0, 32),))
    grain_poses = bell_draw(keys[1], (12, GRAINS), 0.6, 4.0, ((1, 32),), jnp.float32)
    surface_nodes = bell_draw(keys[2], (GRAINS, 3 * NODES), 1.0, 5.0, ((0, 32),), jnp.float32)
    send_list = draw_send_list(jax.random.fold_in(keys[10], 71), 0)
    pair_first = draw_pair_first(jax.random.fold_in(keys[10], 71), 0)
    pair_sdf = draw_pair_sdf(jax.random.fold_in(keys[10], 71), 0)
    pair_pose = draw_pair_pose(jax.random.fold_in(keys[10], 71), 0)
    pair_live = draw_pair_live(jax.random.fold_in(keys[10], 71), 0)
    knot_cells = set_ends(jax.random.randint(keys[8], (PAIRS, 3 * NODES), 1, GRID - 2), jax.random.fold_in(keys[8], 1), 1, (GRID - 2) - 1).astype(jnp.int32)
    offsets = jnp.clip(1.0 * jax.random.uniform(keys[9], (PAIRS, 3 * NODES), jnp.float32) ** steps_of(keys[9], (PAIRS, 3 * NODES), ((0, 32),), -0.2, 0.2), 0.0, 1.0)
    return dict(sdf_grids=sdf_grids, grain_poses=grain_poses, surface_nodes=surface_nodes, send_list=send_list, pair_first=pair_first, pair_sdf=pair_sdf, pair_pose=pair_pose, pair_live=pair_live, knot_cells=knot_cells, offsets=offsets)


DIRECTIONS = ((-1, -1), (-1, 0), (-1, 1), (0, -1), (0, 1), (1, -1), (1, 0), (1, 1))
STIFFNESS = 0.25
pair_block = 32


def spline_tables(knot_cell, fraction):
    complement = 1.0 - fraction
    squared = fraction * fraction
    cubed = squared * fraction
    weights = (complement * complement * complement / 6.0, (3.0 * cubed - 6.0 * squared + 4.0) / 6.0,
               (-3.0 * cubed + 3.0 * squared + 3.0 * fraction + 1.0) / 6.0, cubed / 6.0)
    slopes = (-0.5 * complement * complement, 0.5 * (3.0 * squared - 4.0 * fraction),
              0.5 * (-3.0 * squared + 2.0 * fraction + 1.0), 0.5 * squared)
    cell_ids = jnp.arange(GRID, dtype=jnp.int32)[:, None]
    shape = knot_cell.shape[:2] + (GRID,) + knot_cell.shape[2:]
    basis_rows = jnp.zeros(shape, jnp.float32)
    slope_rows = jnp.zeros(shape, jnp.float32)
    for position in range(4):
        matches = cell_ids == (knot_cell + (position - 1))[:, :, None, :]
        basis_rows = basis_rows + jnp.where(matches, weights[position][:, :, None, :], jnp.float32(0.0))
        slope_rows = slope_rows + jnp.where(matches, slopes[position][:, :, None, :], jnp.float32(0.0))
    return basis_rows, slope_rows


def pair_terms(grid_rows, knot_cell, fraction, pose_first, pose_second, node_body):
    highest = lax.Precision.HIGHEST
    batch_size = grid_rows.shape[0]
    node_count = knot_cell.shape[2]
    basis_rows, slope_rows = spline_tables(knot_cell, fraction)
    x_basis = basis_rows[:, 0].astype(jnp.bfloat16).astype(jnp.float32)
    x_slope = slope_rows[:, 0].astype(jnp.bfloat16).astype(jnp.float32)
    grid_cube = grid_rows.reshape(batch_size, GRID, GRID * GRID).astype(jnp.float32)
    partial_plain = jnp.einsum("pam,pan->pmn", grid_cube, x_basis, precision=highest).reshape(batch_size, GRID, GRID, node_count)
    partial_slope = jnp.einsum("pam,pan->pmn", grid_cube, x_slope, precision=highest).reshape(batch_size, GRID, GRID, node_count)
    basis_y = basis_rows[:, 1]
    slope_y = slope_rows[:, 1]
    section_plain = jnp.einsum("pbcn,pbn->pcn", partial_plain, basis_y, precision=highest)
    section_xslope = jnp.einsum("pbcn,pbn->pcn", partial_slope, basis_y, precision=highest)
    section_yslope = jnp.einsum("pbcn,pbn->pcn", partial_plain, slope_y, precision=highest)
    basis_z = basis_rows[:, 2]
    slope_z = slope_rows[:, 2]
    distance = jnp.einsum("pcn,pcn->pn", section_plain, basis_z, precision=highest)
    gradient = jnp.stack([jnp.einsum("pcn,pcn->pn", section_xslope, basis_z, precision=highest),
                          jnp.einsum("pcn,pcn->pn", section_yslope, basis_z, precision=highest),
                          jnp.einsum("pcn,pcn->pn", section_plain, slope_z, precision=highest)], axis=1)
    penetration = STIFFNESS * jax.nn.relu(-distance)
    rotation_second = pose_second[:, 3:].reshape(batch_size, 3, 3)
    rotation_first = pose_first[:, 3:].reshape(batch_size, 3, 3)
    normal = jnp.einsum("prc,pcn->prn", rotation_second, gradient, precision=highest)
    node_force = penetration[:, None, :] * normal
    lever_arm = jnp.einsum("prc,pcn->prn", rotation_first, node_body, precision=highest)
    net_force = jnp.sum(node_force, axis=2)
    moment = jnp.sum(jnp.cross(lever_arm, node_force, axis=1), axis=2)
    separation = pose_first[:, :3] - pose_second[:, :3]
    moment_other = -(jnp.cross(separation, net_force, axis=1) + moment)
    return jnp.concatenate([net_force, moment], axis=1), jnp.concatenate([-net_force, moment_other], axis=1)


def pair_loads(grid_table, pose_table, grain_poses, surface_nodes, pair_first, pair_sdf, pair_pose, pair_live, knot_cells, offsets):
    pair_count = pair_first.shape[0]
    node_count = knot_cells.shape[1] // 3
    block_size = min(pair_block, pair_count)
    grid_rows = jnp.take(grid_table, pair_sdf, axis=0)
    pose_first = jnp.take(grain_poses, pair_first, axis=1).T
    pose_second = jnp.take(pose_table, pair_pose, axis=1).T
    node_body = jnp.take(surface_nodes, pair_first, axis=0).reshape(pair_count, 3, node_count)
    knot_cell = knot_cells.reshape(pair_count, 3, node_count)
    fraction = offsets.reshape(pair_count, 3, node_count)
    pieces = (grid_rows, knot_cell, fraction, pose_first, pose_second, node_body)
    blocked = tuple(item.reshape((pair_count // block_size, block_size) + item.shape[1:]) for item in pieces)
    on_first, on_second = lax.map(lambda group: pair_terms(*group), blocked)
    alive_mask = pair_live.astype(jnp.float32)[:, None]
    on_first = on_first.reshape(pair_count, 6) * alive_mask
    on_second = on_second.reshape(pair_count, 6) * alive_mask
    return jax.ops.segment_sum(jnp.concatenate([on_first, on_second], axis=0),
                               jnp.concatenate([pair_first, pair_sdf], axis=0).astype(jnp.int32),
                               num_segments=grid_table.shape[0])


def shift_grid(field, row_step, col_step):
    padded = jnp.pad(field, ((1, 1), (1, 1)) + ((0, 0),) * (field.ndim - 2))
    return padded[1 + row_step:1 + row_step + N_ROW, 1 + col_step:1 + col_step + N_COL]


def reference(sdf_grids, grain_poses, surface_nodes, send_list, pair_first, pair_sdf, pair_pose, pair_live, knot_cells, offsets):
    devices = N_ROW * N_COL
    cells = sdf_grids.shape[1]
    grids_dev = sdf_grids.reshape(devices, GR_DEV, cells)
    listed = send_list.reshape(devices, 8 * GHOST)
    outgoing = jax.vmap(lambda grid_set, chosen: jnp.take(grid_set, chosen, axis=0))(grids_dev, listed)
    outgoing = outgoing.reshape(N_ROW, N_COL, 8, GHOST, cells)
    received = jnp.stack([shift_grid(outgoing[:, :, 7 - direction], DIRECTIONS[direction][0], DIRECTIONS[direction][1])
                          for direction in range(8)], axis=2)
    grid_table = jnp.concatenate([grids_dev.reshape(N_ROW, N_COL, GR_DEV, cells),
                                  received.reshape(N_ROW, N_COL, 8 * GHOST, cells)], axis=2)
    grid_table = grid_table.reshape(devices, GR_DEV + 8 * GHOST, cells)
    pose_dev = grain_poses.reshape(12, N_ROW, N_COL, GR_DEV).transpose(1, 2, 0, 3)
    pose_table = jnp.stack([shift_grid(pose_dev, row_step, col_step) for row_step in (-1, 0, 1) for col_step in (-1, 0, 1)], axis=3)
    pose_table = pose_table.reshape(devices, 12, 9 * GR_DEV)
    slot_sums = lax.map(lambda pieces: pair_loads(*pieces),
                        (grid_table, pose_table, pose_dev.reshape(devices, 12, GR_DEV),
                         surface_nodes.reshape(devices, GR_DEV, -1), pair_first.reshape(devices, -1),
                         pair_sdf.reshape(devices, -1), pair_pose.reshape(devices, -1), pair_live.reshape(devices, -1),
                         knot_cells.reshape(devices, PAIRS_DEV, -1), offsets.reshape(devices, PAIRS_DEV, -1)))
    owned_sum = slot_sums[:, :GR_DEV]
    reaction = slot_sums[:, GR_DEV:].reshape(N_ROW, N_COL, 8, GHOST, 6)
    returned = jnp.stack([shift_grid(reaction[:, :, 7 - direction], DIRECTIONS[direction][0], DIRECTIONS[direction][1])
                          for direction in range(8)], axis=2).reshape(devices, 8 * GHOST, 6)
    owned_sum = owned_sum + jax.vmap(lambda loads, chosen: jax.ops.segment_sum(loads, chosen, num_segments=GR_DEV))(returned, listed)
    return owned_sum.transpose(2, 0, 1).reshape(6, devices * GR_DEV)
```

```python
import functools

import jax
import jax.numpy as jnp
from jax import lax
from jax.experimental import pallas as pl
from jax.experimental.pallas import tpu as pltpu
from jax.sharding import PartitionSpec as P

GRID = 16
DIRECTIONS = ((-1, -1), (-1, 0), (-1, 1), (0, -1), (0, 1), (1, -1), (1, 0), (1, 1))
STIFFNESS = 0.25
CHUNKS = 4
MESH = pl.DeviceIdType.MESH
HIGHEST = lax.Precision.HIGHEST
F32 = jnp.float32
BF16 = jnp.bfloat16


def spline(knot, frac, rows):
    cell = lax.broadcasted_iota(jnp.int32, (rows, knot.shape[1]), 0).astype(F32)
    t = (knot - cell) + frac
    s = jnp.abs(t)
    p = jnp.maximum(2.0 - s, 0.0)
    q = jnp.maximum(1.0 - s, 0.0)
    p2 = p * p
    q2 = q * q
    basis = (p2 * p) * (1.0 / 6.0) - (q2 * q) * (4.0 / 6.0)
    down = 2.0 * q2 - 0.5 * p2
    slope = jnp.where(t < 0.0, -down, down)
    return basis, slope


def kernel(
    n_row, n_col, stored,
    grids, poses, nodes, lists, rows, knots, offsets,
    out,
    send_buf, ghost, pose_out, pose_in, react, ret, cube, weights, fields, lever,
    send_sem, recv_sem, psend_sem, precv_sem, rsend_sem, rrecv_sem,
):
    r = lax.axis_index("row")
    c = lax.axis_index("col")
    grains = grids.shape[0]
    capacity = lists.shape[1]
    pairs = knots.shape[0]
    count = knots.shape[1] // 3
    plane = GRID * GRID
    slots = 8 * capacity
    width = grids.shape[1] // CHUNKS

    def there(d):
        dr, dc = DIRECTIONS[d]
        rr, cc = r + dr, c + dc
        ok = (rr >= 0) & (rr < n_row) & (cc >= 0) & (cc < n_col)
        return ok, (rr, cc)

    peers = sum(there(d)[0].astype(jnp.int32) for d in range(8))
    barrier = pltpu.get_barrier_semaphore()
    for d in range(8):
        ok, place = there(d)

        @pl.when(ok)
        def _():
            pl.semaphore_signal(barrier, inc=1, device_id=place, device_id_type=MESH)

        @pl.when(jnp.logical_not(ok))
        def _():
            ghost[d * capacity:(d + 1) * capacity, :] = jnp.zeros((capacity, grids.shape[1]), BF16)
            pose_in[d] = jnp.zeros(pose_in.shape[1:], F32)
            ret[d] = jnp.zeros(ret.shape[1:], F32)

    columns = rows[...].astype(F32).T
    send_col = columns[:, 0:1]
    first_col = columns[:pairs, 1:2]
    sdf_col = columns[:pairs, 2:3]
    first_row = rows[1:2, :pairs]
    sdf_row = rows[2:3, :pairs]
    live_row = rows[3:4, :pairs].astype(F32)

    lane_grains = lax.broadcasted_iota(jnp.int32, (1, grains), 1).astype(F32)
    oh_send = jnp.where(send_col == lane_grains, 1.0, 0.0).astype(BF16)

    pose_out[...] = jnp.zeros(pose_out.shape, F32)
    sub_grains = lax.broadcasted_iota(jnp.int32, (grains, 1), 0)
    for d in range(8):
        picked = jnp.where(lists[d:d + 1, :] == sub_grains, 1.0, 0.0)
        pose_out[d, 0:12, 0:capacity] = jnp.dot(
            poses[...], picked, preferred_element_type=F32, precision=HIGHEST)

    def pose_copy(d):
        return pltpu.make_async_remote_copy(
            src_ref=pose_out.at[d], dst_ref=pose_in.at[7 - d],
            send_sem=psend_sem.at[d], recv_sem=precv_sem.at[7 - d],
            device_id=there(d)[1], device_id_type=MESH)

    def grid_copy(d, k):
        return pltpu.make_async_remote_copy(
            src_ref=send_buf.at[pl.ds(d * capacity, capacity), pl.ds(k * width, width)],
            dst_ref=ghost.at[pl.ds((7 - d) * capacity, capacity), pl.ds(k * width, width)],
            send_sem=send_sem.at[d, k], recv_sem=recv_sem.at[7 - d, k],
            device_id=there(d)[1], device_id_type=MESH)

    def react_copy(d):
        return pltpu.make_async_remote_copy(
            src_ref=react.at[d], dst_ref=ret.at[7 - d],
            send_sem=rsend_sem.at[d], recv_sem=rrecv_sem.at[7 - d],
            device_id=there(d)[1], device_id_type=MESH)

    order = (0, 2, 5, 7, 3, 4, 1, 6)
    for k in range(CHUNKS):
        def gather(j, carry, k=k):
            at = pl.ds(pl.multiple_of(k * width + j * plane, plane), plane)
            send_buf[:, at] = jnp.dot(
                oh_send, grids[:, at], preferred_element_type=F32).astype(BF16)
            return carry

        lax.fori_loop(0, width // plane, gather, 0)
        if k == 0:
            pl.semaphore_wait(barrier, peers)
        for d in order:
            @pl.when(there(d)[0])
            def _():
                grid_copy(d, k).start()
    for d in range(8):
        @pl.when(there(d)[0])
        def _():
            pose_copy(d).start()

    oh_own = jnp.where(sdf_col == lane_grains, 1.0, 0.0).astype(BF16)
    oh_first = jnp.where(first_col == lane_grains, 1.0, 0.0).astype(BF16)

    def own_cube(a, carry):
        at = pl.ds(pl.multiple_of(a * plane, plane), plane)
        found = jnp.dot(oh_own, grids[:, at], preferred_element_type=F32)
        for h in range(plane // 128):
            cube[h, pl.ds(a, pairs, stride=GRID), :] = found[:, h * 128:(h + 1) * 128]
        return carry

    lax.fori_loop(0, GRID, own_cube, 0)

    body = nodes[...]
    high = body.astype(BF16)
    low = (body - high.astype(F32)).astype(BF16)
    lever[...] = (jnp.dot(oh_first, high, preferred_element_type=F32)
                  + jnp.dot(oh_first, low, preferred_element_type=F32))

    def pair_weights(p, slot):
        knot = knots[pl.ds(p, 1), :].astype(F32)
        frac = offsets[pl.ds(p, 1), :]
        by, sy = spline(knot[:, count:2 * count], frac[:, count:2 * count], GRID)
        bz, sz = spline(knot[:, 2 * count:], frac[:, 2 * count:], GRID)
        for b in range(GRID):
            y = by[b:b + 1, :]
            weights[slot, b * GRID:(b + 1) * GRID, 0:count] = (y * bz).astype(BF16)
            weights[slot, b * GRID:(b + 1) * GRID, count:2 * count] = (
                sy[b:b + 1, :] * bz).astype(BF16)
            weights[slot, b * GRID:(b + 1) * GRID, 2 * count:] = (y * sz).astype(BF16)

    def build(p, carry):
        pair_weights(p, p)
        return carry

    lax.fori_loop(0, stored, build, 0)

    for d in range(8):
        @pl.when(there(d)[0])
        def _():
            pose_copy(d).wait_send()
            for k in range(CHUNKS):
                grid_copy(d, k).wait_send()

        back = 7 - d

        @pl.when(there(d)[0])
        def _():
            pltpu.make_async_remote_copy(
                src_ref=pose_out.at[back], dst_ref=pose_in.at[d],
                send_sem=psend_sem.at[back], recv_sem=precv_sem.at[d],
                device_id=there(d)[1], device_id_type=MESH).wait_recv()
            for k in range(CHUNKS):
                pltpu.make_async_remote_copy(
                    src_ref=send_buf.at[pl.ds(back * capacity, capacity), pl.ds(k * width, width)],
                    dst_ref=ghost.at[pl.ds(d * capacity, capacity), pl.ds(k * width, width)],
                    send_sem=send_sem.at[back, k], recv_sem=recv_sem.at[d, k],
                    device_id=there(d)[1], device_id_type=MESH).wait_recv()

    lane_slots = lax.broadcasted_iota(jnp.int32, (1, slots), 1).astype(F32)
    oh_ghost = jnp.where(sdf_col - float(grains) == lane_slots, 1.0, 0.0).astype(BF16)

    def ghost_cube(a, carry):
        at = pl.ds(pl.multiple_of(a * plane, plane), plane)
        found = jnp.dot(oh_ghost, ghost[:, at], preferred_element_type=F32)
        for h in range(plane // 128):
            cube[h, pl.ds(a, pairs, stride=GRID), :] += found[:, h * 128:(h + 1) * 128]
        return carry

    lax.fori_loop(0, GRID, ghost_cube, 0)

    def pair_fields(p, slot):
        knot = knots[pl.ds(p, 1), :].astype(F32)
        frac = offsets[pl.ds(p, 1), :]
        bx, sx = spline(knot[:, :count], frac[:, :count], GRID)
        bx = bx.astype(BF16).astype(F32)
        sx = sx.astype(BF16).astype(F32)
        at = pl.ds(pl.multiple_of(p * GRID, GRID), GRID)
        g = jnp.concatenate([cube[0, at, :], cube[1, at, :]], axis=1).astype(BF16)
        s = jnp.dot(g, weights[slot], preferred_element_type=F32)
        plain = s[:, :count]
        fields[0, pl.ds(p, 1), :] = jnp.sum(plain * bx, axis=0, keepdims=True)
        fields[1, pl.ds(p, 1), :] = jnp.sum(plain * sx, axis=0, keepdims=True)
        fields[2, pl.ds(p, 1), :] = jnp.sum(s[:, count:2 * count] * bx, axis=0, keepdims=True)
        fields[3, pl.ds(p, 1), :] = jnp.sum(s[:, 2 * count:] * bx, axis=0, keepdims=True)

    def contract(i, carry):
        for u in range(4):
            pair_fields(i * 4 + u, i * 4 + u)
        return carry

    lax.fori_loop(0, stored // 4, contract, 0)

    def late(p, carry):
        pair_weights(p, p - stored)
        pair_fields(p, p - stored)
        return carry

    if stored < pairs:
        lax.fori_loop(stored, pairs, late, 0)

    push = STIFFNESS * jnp.maximum(-fields[0], 0.0)
    lane = lax.broadcasted_iota(jnp.int32, (pairs, 128), 1)
    gathered = jnp.zeros((pairs, 128), F32)
    for k in range(3):
        g = push * fields[1 + k]
        gathered = jnp.where(lane == k, jnp.sum(g, axis=1, keepdims=True), gathered)
        for i in range(3):
            moved = jnp.sum(g * lever[:, i * count:(i + 1) * count], axis=1, keepdims=True)
            gathered = jnp.where(lane == 3 + 3 * i + k, moved, gathered)
    sums = gathered.T

    own_first = jnp.where(first_row == sub_grains, 1.0, 0.0)
    own_second = jnp.where(sdf_row == sub_grains, 1.0, 0.0)
    pose1 = jnp.dot(poses[...], own_first, preferred_element_type=F32, precision=HIGHEST)
    pose2 = jnp.dot(poses[...], own_second, preferred_element_type=F32, precision=HIGHEST)
    sub_cap = lax.broadcasted_iota(jnp.int32, (capacity, 1), 0)
    for d in range(8):
        picked = jnp.where(sdf_row - (grains + d * capacity) == sub_cap, 1.0, 0.0)
        pose2 = pose2 + jnp.dot(
            pose_in[d, 0:12, 0:capacity], picked, preferred_element_type=F32, precision=HIGHEST)

    def rot(pose, i, j):
        k = 3 + 3 * i + j
        return pose[k:k + 1, :]

    total = [sums[k:k + 1, :] for k in range(3)]
    force = [sum(rot(pose2, i, j) * total[j] for j in range(3)) for i in range(3)]
    half = [[sum(sums[3 + 3 * i + j:4 + 3 * i + j, :] * rot(pose2, s, j) for j in range(3))
             for s in range(3)] for i in range(3)]
    full = [[sum(rot(pose1, q, i) * half[i][s] for i in range(3)) for s in range(3)]
            for q in range(3)]
    moment = [full[1][2] - full[2][1], full[2][0] - full[0][2], full[0][1] - full[1][0]]
    apart = [pose1[k:k + 1, :] - pose2[k:k + 1, :] for k in range(3)]
    other = [-(apart[1] * force[2] - apart[2] * force[1] + moment[0]),
             -(apart[2] * force[0] - apart[0] * force[2] + moment[1]),
             -(apart[0] * force[1] - apart[1] * force[0] + moment[2])]
    blank = jnp.zeros((2, pairs), F32)
    on_first = jnp.concatenate(force + moment + [blank], axis=0) * live_row
    on_second = jnp.concatenate([-f for f in force] + other + [blank], axis=0) * live_row

    lane_ret = lax.broadcasted_iota(jnp.int32, (1, react.shape[2]), 1).astype(F32)
    for d in range(8):
        picked = jnp.where(sdf_col - float(grains + d * capacity) == lane_ret, 1.0, 0.0)
        react[d] = jnp.dot(on_second, picked, preferred_element_type=F32, precision=HIGHEST)

        @pl.when(there(d)[0])
        def _():
            react_copy(d).start()

    loads = (jnp.dot(on_first, oh_first.astype(F32), preferred_element_type=F32, precision=HIGHEST)
             + jnp.dot(on_second, oh_own.astype(F32), preferred_element_type=F32, precision=HIGHEST))
    for d in range(8):
        back = 7 - d

        @pl.when(there(d)[0])
        def _():
            react_copy(d).wait_send()
            pltpu.make_async_remote_copy(
                src_ref=react.at[back], dst_ref=ret.at[d],
                send_sem=rsend_sem.at[back], recv_sem=rrecv_sem.at[d],
                device_id=there(d)[1], device_id_type=MESH).wait_recv()

        picked = jnp.where(send_col[d * capacity:(d + 1) * capacity, :] == lane_grains, 1.0, 0.0)
        loads = loads + jnp.dot(
            ret[d][:, 0:capacity], picked, preferred_element_type=F32, precision=HIGHEST)
    out[...] = loads[0:6, :]


def local(
    n_row, n_col,
    sdf_grids, grain_poses, surface_nodes, send_list,
    pair_first, pair_sdf, pair_pose, pair_live, knot_cells, offsets,
):
    grains, cells = sdf_grids.shape
    capacity = send_list.shape[3]
    pairs = pair_first.shape[0]
    slots = 8 * capacity
    count = knot_cells.shape[1] // 3
    stored = min(pairs, 96)
    lists = send_list.reshape(8, capacity)
    span = max(slots, pairs)
    rows = jnp.stack([
        jnp.pad(v, (0, span - v.shape[0]))
        for v in (lists.reshape(-1), pair_first, pair_sdf, pair_live)
    ] + [jnp.zeros((span,), jnp.int32)] * 4)
    vmem = pl.BlockSpec(memory_space=pltpu.VMEM)
    return pl.pallas_call(
        functools.partial(kernel, n_row, n_col, stored),
        out_shape=jax.ShapeDtypeStruct((6, grains), F32),
        in_specs=[vmem] * 7,
        out_specs=vmem,
        scratch_shapes=[
            pltpu.VMEM((slots, cells), BF16),
            pltpu.VMEM((slots, cells), BF16),
            pltpu.VMEM((8, 16, 128), F32),
            pltpu.VMEM((8, 16, 128), F32),
            pltpu.VMEM((8, 8, 128), F32),
            pltpu.VMEM((8, 8, 128), F32),
            pltpu.VMEM((GRID * GRID // 128, pairs * GRID, 128), F32),
            pltpu.VMEM((stored, GRID * GRID, 3 * count), BF16),
            pltpu.VMEM((4, pairs, count), F32),
            pltpu.VMEM((pairs, 3 * count), F32),
            pltpu.SemaphoreType.DMA((8, CHUNKS)),
            pltpu.SemaphoreType.DMA((8, CHUNKS)),
            pltpu.SemaphoreType.DMA((8,)),
            pltpu.SemaphoreType.DMA((8,)),
            pltpu.SemaphoreType.DMA((8,)),
            pltpu.SemaphoreType.DMA((8,)),
        ],
        compiler_params=pltpu.CompilerParams(
            collective_id=0, has_side_effects=True, vmem_limit_bytes=60 * 2**20),
    )(sdf_grids, grain_poses, surface_nodes, lists, rows, knot_cells, offsets)


def solution(mesh):
    in_specs = (
        P(("row", "col"), None),
        P(None, ("row", "col")),
        P(("row", "col"), None),
        P("row", "col", None, None),
        P(("row", "col")),
        P(("row", "col")),
        P(("row", "col")),
        P(("row", "col")),
        P(("row", "col"), None),
        P(("row", "col"), None),
    )
    out_specs = P(None, ("row", "col"))
    body = functools.partial(local, mesh.shape["row"], mesh.shape["col"])
    return jax.shard_map(body, mesh=mesh, in_specs=in_specs, out_specs=out_specs, check_vma=False)
```

```python
import functools

import jax
import jax.numpy as jnp
from jax import lax
from jax.experimental import pallas as pl
from jax.experimental.pallas import tpu as pltpu
from jax.sharding import PartitionSpec as P

GRID = 16
DIRECTIONS = ((-1, -1), (-1, 0), (-1, 1), (0, -1), (0, 1), (1, -1), (1, 0), (1, 1))
STIFFNESS = 0.25
CHUNKS = 4
MESH = pl.DeviceIdType.MESH
HIGHEST = lax.Precision.HIGHEST
F32 = jnp.float32
BF16 = jnp.bfloat16


def spline(knot, frac, rows):
    cell = lax.broadcasted_iota(jnp.int32, (rows, knot.shape[1]), 0).astype(F32)
    t = (knot - cell) + frac
    s = jnp.abs(t)
    p = jnp.maximum(2.0 - s, 0.0)
    q = jnp.maximum(1.0 - s, 0.0)
    p2 = p * p
    q2 = q * q
    basis = (p2 * p) * (1.0 / 6.0) - (q2 * q) * (4.0 / 6.0)
    down = 2.0 * q2 - 0.5 * p2
    slope = jnp.where(t < 0.0, -down, down)
    return basis, slope


def kernel(
    n_row, n_col, stored,
    grids, poses, nodes, lists, first, second, live, knots, offsets,
    out,
    send_buf, ghost, pose_out, pose_in, react, ret, cube, weights, fields, lever,
    send_sem, recv_sem, psend_sem, precv_sem, rsend_sem, rrecv_sem,
):
    r = lax.axis_index("row")
    c = lax.axis_index("col")
    grains = grids.shape[0]
    capacity = lists.shape[1]
    pairs = knots.shape[0]
    count = knots.shape[1] // 3
    plane = GRID * GRID
    slots = 8 * capacity
    width = grids.shape[1] // CHUNKS

    def there(d):
        dr, dc = DIRECTIONS[d]
        rr, cc = r + dr, c + dc
        ok = (rr >= 0) & (rr < n_row) & (cc >= 0) & (cc < n_col)
        return ok, (rr, cc)

    peers = sum(there(d)[0].astype(jnp.int32) for d in range(8))
    barrier = pltpu.get_barrier_semaphore()
    for d in range(8):
        ok, place = there(d)

        @pl.when(ok)
        def _():
            pl.semaphore_signal(barrier, inc=1, device_id=place, device_id_type=MESH)

        @pl.when(jnp.logical_not(ok))
        def _():
            ghost[d * capacity:(d + 1) * capacity, :] = jnp.zeros((capacity, grids.shape[1]), BF16)
            pose_in[d] = jnp.zeros(pose_in.shape[1:], F32)
            ret[d] = jnp.zeros(ret.shape[1:], F32)

    first_row = first[...]
    sdf_row = second[...]
    live_row = live[...].astype(F32)
    stacked = jnp.concatenate(
        [first_row.astype(F32), sdf_row.astype(F32), jnp.zeros((6, pairs), F32)], axis=0).T
    first_col = stacked[:, 0:1]
    sdf_col = stacked[:, 1:2]
    spare = jnp.zeros((8, -capacity % 128), F32)
    turned = jnp.concatenate([lists[...].astype(F32), spare], axis=1).T
    send_col = jnp.concatenate([turned[:capacity, d:d + 1] for d in range(8)], axis=0)

    lane_grains = lax.broadcasted_iota(jnp.int32, (1, grains), 1).astype(F32)
    oh_send = jnp.where(send_col == lane_grains, 1.0, 0.0).astype(BF16)

    pose_out[...] = jnp.zeros(pose_out.shape, F32)
    sub_grains = lax.broadcasted_iota(jnp.int32, (grains, 1), 0)
    for d in range(8):
        picked = jnp.where(lists[d:d + 1, :] == sub_grains, 1.0, 0.0)
        pose_out[d, 0:12, 0:capacity] = jnp.dot(
            poses[...], picked, preferred_element_type=F32, precision=HIGHEST)

    def pose_copy(d):
        return pltpu.make_async_remote_copy(
            src_ref=pose_out.at[d], dst_ref=pose_in.at[7 - d],
            send_sem=psend_sem.at[d], recv_sem=precv_sem.at[7 - d],
            device_id=there(d)[1], device_id_type=MESH)

    def grid_copy(d, k):
        return pltpu.make_async_remote_copy(
            src_ref=send_buf.at[pl.ds(d * capacity, capacity), pl.ds(k * width, width)],
            dst_ref=ghost.at[pl.ds((7 - d) * capacity, capacity), pl.ds(k * width, width)],
            send_sem=send_sem.at[d, k], recv_sem=recv_sem.at[7 - d, k],
            device_id=there(d)[1], device_id_type=MESH)

    def react_copy(d):
        return pltpu.make_async_remote_copy(
            src_ref=react.at[d], dst_ref=ret.at[7 - d],
            send_sem=rsend_sem.at[d], recv_sem=rrecv_sem.at[7 - d],
            device_id=there(d)[1], device_id_type=MESH)

    order = (0, 2, 5, 7, 3, 4, 1, 6)
    for k in range(CHUNKS):
        def gather(j, carry, k=k):
            at = pl.ds(pl.multiple_of(k * width + j * plane, plane), plane)
            send_buf[:, at] = jnp.dot(
                oh_send, grids[:, at], preferred_element_type=F32).astype(BF16)
            return carry

        lax.fori_loop(0, width // plane, gather, 0, unroll=True)
        if k == 0:
            pl.semaphore_wait(barrier, peers)
        for d in order:
            @pl.when(there(d)[0])
            def _():
                grid_copy(d, k).start()
    for d in range(8):
        @pl.when(there(d)[0])
        def _():
            pose_copy(d).start()

    oh_own = jnp.where(sdf_col == lane_grains, 1.0, 0.0).astype(BF16)
    oh_first = jnp.where(first_col == lane_grains, 1.0, 0.0).astype(BF16)

    def own_cube(a, carry):
        at = pl.ds(pl.multiple_of(a * plane, plane), plane)
        found = jnp.dot(oh_own, grids[:, at], preferred_element_type=F32)
        for h in range(plane // 128):
            cube[h, pl.ds(pl.multiple_of(a * pairs, pairs), pairs), :] = found[:, h * 128:(h + 1) * 128]
        return carry

    lax.fori_loop(0, GRID, own_cube, 0, unroll=4)

    body = nodes[...]
    high = body.astype(BF16)
    low = (body - high.astype(F32)).astype(BF16)
    lever[...] = (jnp.dot(oh_first, high, preferred_element_type=F32)
                  + jnp.dot(oh_first, low, preferred_element_type=F32))

    def pair_weights(p, slot):
        knot = knots[pl.ds(p, 1), :].astype(F32)
        frac = offsets[pl.ds(p, 1), :]
        by, sy = spline(knot[:, count:2 * count], frac[:, count:2 * count], GRID)
        bz, sz = spline(knot[:, 2 * count:], frac[:, 2 * count:], GRID)
        for b in range(GRID):
            y = by[b:b + 1, :]
            weights[slot, b * GRID:(b + 1) * GRID, 0:count] = (y * bz).astype(BF16)
            weights[slot, b * GRID:(b + 1) * GRID, count:2 * count] = (
                sy[b:b + 1, :] * bz).astype(BF16)
            weights[slot, b * GRID:(b + 1) * GRID, 2 * count:] = (y * sz).astype(BF16)

    def build(p, carry):
        pair_weights(p, p)
        return carry

    lax.fori_loop(0, stored, build, 0)

    for d in range(8):
        @pl.when(there(d)[0])
        def _():
            pose_copy(d).wait_send()
            for k in range(CHUNKS):
                grid_copy(d, k).wait_send()

        back = 7 - d

        @pl.when(there(d)[0])
        def _():
            pltpu.make_async_remote_copy(
                src_ref=pose_out.at[back], dst_ref=pose_in.at[d],
                send_sem=psend_sem.at[back], recv_sem=precv_sem.at[d],
                device_id=there(d)[1], device_id_type=MESH).wait_recv()
            for k in range(CHUNKS):
                pltpu.make_async_remote_copy(
                    src_ref=send_buf.at[pl.ds(back * capacity, capacity), pl.ds(k * width, width)],
                    dst_ref=ghost.at[pl.ds(d * capacity, capacity), pl.ds(k * width, width)],
                    send_sem=send_sem.at[back, k], recv_sem=recv_sem.at[d, k],
                    device_id=there(d)[1], device_id_type=MESH).wait_recv()

    lane_slots = lax.broadcasted_iota(jnp.int32, (1, slots), 1).astype(F32)
    oh_ghost = jnp.where(sdf_col - float(grains) == lane_slots, 1.0, 0.0).astype(BF16)

    def ghost_cube(a, carry):
        at = pl.ds(pl.multiple_of(a * plane, plane), plane)
        found = jnp.dot(oh_ghost, ghost[:, at], preferred_element_type=F32)
        for h in range(plane // 128):
            cube[h, pl.ds(pl.multiple_of(a * pairs, pairs), pairs), :] += found[:, h * 128:(h + 1) * 128]
        return carry

    lax.fori_loop(0, GRID, ghost_cube, 0, unroll=4)

    def pair_fields(p, slot):
        knot = knots[pl.ds(p, 1), :].astype(F32)
        frac = offsets[pl.ds(p, 1), :]
        bx, sx = spline(knot[:, :count], frac[:, :count], GRID)
        bx = bx.astype(BF16).astype(F32)
        sx = sx.astype(BF16).astype(F32)
        at = pl.ds(p, GRID, stride=pairs)
        g = jnp.concatenate([cube[0, at, :], cube[1, at, :]], axis=1).astype(BF16)
        s = jnp.dot(g, weights[slot], preferred_element_type=F32)
        plain = s[:, :count]
        fields[0, pl.ds(p, 1), :] = jnp.sum(plain * bx, axis=0, keepdims=True)
        fields[1, pl.ds(p, 1), :] = jnp.sum(plain * sx, axis=0, keepdims=True)
        fields[2, pl.ds(p, 1), :] = jnp.sum(s[:, count:2 * count] * bx, axis=0, keepdims=True)
        fields[3, pl.ds(p, 1), :] = jnp.sum(s[:, 2 * count:] * bx, axis=0, keepdims=True)

    def contract(i, carry):
        for u in range(8):
            pair_fields(i * 8 + u, i * 8 + u)
        return carry

    lax.fori_loop(0, stored // 8, contract, 0)

    def late(i, carry):
        for u in range(4):
            pair_weights(stored + i * 4 + u, i * 4 + u)
        for u in range(4):
            pair_fields(stored + i * 4 + u, i * 4 + u)
        return carry

    if stored < pairs:
        lax.fori_loop(0, (pairs - stored) // 4, late, 0)

    push = STIFFNESS * jnp.maximum(-fields[0], 0.0)
    lane = lax.broadcasted_iota(jnp.int32, (pairs, 128), 1)
    gathered = jnp.zeros((pairs, 128), F32)
    for k in range(3):
        g = push * fields[1 + k]
        gathered = jnp.where(lane == k, jnp.sum(g, axis=1, keepdims=True), gathered)
        for i in range(3):
            moved = jnp.sum(g * lever[:, i * count:(i + 1) * count], axis=1, keepdims=True)
            gathered = jnp.where(lane == 3 + 3 * i + k, moved, gathered)
    sums = gathered.T

    own_first = jnp.where(first_row == sub_grains, 1.0, 0.0)
    own_second = jnp.where(sdf_row == sub_grains, 1.0, 0.0)
    pose1 = jnp.dot(poses[...], own_first, preferred_element_type=F32, precision=HIGHEST)
    pose2 = jnp.dot(poses[...], own_second, preferred_element_type=F32, precision=HIGHEST)
    sub_cap = lax.broadcasted_iota(jnp.int32, (capacity, 1), 0)
    for d in range(8):
        picked = jnp.where(sdf_row - (grains + d * capacity) == sub_cap, 1.0, 0.0)
        pose2 = pose2 + jnp.dot(
            pose_in[d, 0:12, 0:capacity], picked, preferred_element_type=F32, precision=HIGHEST)

    def rot(pose, i, j):
        k = 3 + 3 * i + j
        return pose[k:k + 1, :]

    total = [sums[k:k + 1, :] for k in range(3)]
    force = [sum(rot(pose2, i, j) * total[j] for j in range(3)) for i in range(3)]
    half = [[sum(sums[3 + 3 * i + j:4 + 3 * i + j, :] * rot(pose2, s, j) for j in range(3))
             for s in range(3)] for i in range(3)]
    full = [[sum(rot(pose1, q, i) * half[i][s] for i in range(3)) for s in range(3)]
            for q in range(3)]
    moment = [full[1][2] - full[2][1], full[2][0] - full[0][2], full[0][1] - full[1][0]]
    apart = [pose1[k:k + 1, :] - pose2[k:k + 1, :] for k in range(3)]
    other = [-(apart[1] * force[2] - apart[2] * force[1] + moment[0]),
             -(apart[2] * force[0] - apart[0] * force[2] + moment[1]),
             -(apart[0] * force[1] - apart[1] * force[0] + moment[2])]
    blank = jnp.zeros((2, pairs), F32)
    on_first = jnp.concatenate(force + moment + [blank], axis=0) * live_row
    on_second = jnp.concatenate([-f for f in force] + other + [blank], axis=0) * live_row

    lane_ret = lax.broadcasted_iota(jnp.int32, (1, react.shape[2]), 1).astype(F32)
    for d in range(8):
        picked = jnp.where(sdf_col - float(grains + d * capacity) == lane_ret, 1.0, 0.0)
        react[d] = jnp.dot(on_second, picked, preferred_element_type=F32, precision=HIGHEST)

        @pl.when(there(d)[0])
        def _():
            react_copy(d).start()

    loads = (jnp.dot(on_first, oh_first.astype(F32), preferred_element_type=F32, precision=HIGHEST)
             + jnp.dot(on_second, oh_own.astype(F32), preferred_element_type=F32, precision=HIGHEST))
    for d in range(8):
        back = 7 - d

        @pl.when(there(d)[0])
        def _():
            react_copy(d).wait_send()
            pltpu.make_async_remote_copy(
                src_ref=react.at[back], dst_ref=ret.at[d],
                send_sem=rsend_sem.at[back], recv_sem=rrecv_sem.at[d],
                device_id=there(d)[1], device_id_type=MESH).wait_recv()

        picked = jnp.where(send_col[d * capacity:(d + 1) * capacity, :] == lane_grains, 1.0, 0.0)
        loads = loads + jnp.dot(
            ret[d][:, 0:capacity], picked, preferred_element_type=F32, precision=HIGHEST)
    out[...] = loads[0:6, :]


def local(
    n_row, n_col,
    sdf_grids, grain_poses, surface_nodes, send_list,
    pair_first, pair_sdf, pair_pose, pair_live, knot_cells, offsets,
):
    grains, cells = sdf_grids.shape
    capacity = send_list.shape[3]
    pairs = pair_first.shape[0]
    slots = 8 * capacity
    count = knot_cells.shape[1] // 3
    stored = min(pairs, 112)
    lists = send_list.reshape(8, capacity)
    vmem = pl.BlockSpec(memory_space=pltpu.VMEM)
    return pl.pallas_call(
        functools.partial(kernel, n_row, n_col, stored),
        out_shape=jax.ShapeDtypeStruct((6, grains), F32),
        in_specs=[vmem] * 9,
        out_specs=vmem,
        scratch_shapes=[
            pltpu.VMEM((slots, cells), BF16),
            pltpu.VMEM((slots, cells), BF16),
            pltpu.VMEM((8, 16, 128), F32),
            pltpu.VMEM((8, 16, 128), F32),
            pltpu.VMEM((8, 8, 128), F32),
            pltpu.VMEM((8, 8, 128), F32),
            pltpu.VMEM((GRID * GRID // 128, pairs * GRID, 128), F32),
            pltpu.VMEM((stored, GRID * GRID, 3 * count), BF16),
            pltpu.VMEM((4, pairs, count), F32),
            pltpu.VMEM((pairs, 3 * count), F32),
            pltpu.SemaphoreType.DMA((8, CHUNKS)),
            pltpu.SemaphoreType.DMA((8, CHUNKS)),
            pltpu.SemaphoreType.DMA((8,)),
            pltpu.SemaphoreType.DMA((8,)),
            pltpu.SemaphoreType.DMA((8,)),
            pltpu.SemaphoreType.DMA((8,)),
        ],
        compiler_params=pltpu.CompilerParams(
            collective_id=0, has_side_effects=True, vmem_limit_bytes=62 * 2**20),
    )(sdf_grids, grain_poses, surface_nodes, lists, pair_first.reshape(1, pairs),
      pair_sdf.reshape(1, pairs), pair_live.reshape(1, pairs), knot_cells, offsets)


def solution(mesh):
    in_specs = (
        P(("row", "col"), None),
        P(None, ("row", "col")),
        P(("row", "col"), None),
        P("row", "col", None, None),
        P(("row", "col")),
        P(("row", "col")),
        P(("row", "col")),
        P(("row", "col")),
        P(("row", "col"), None),
        P(("row", "col"), None),
    )
    out_specs = P(None, ("row", "col"))
    body = functools.partial(local, mesh.shape["row"], mesh.shape["col"])
    return jax.shard_map(body, mesh=mesh, in_specs=in_specs, out_specs=out_specs, check_vma=False)
```

```python
import functools

import jax
import jax.numpy as jnp
from jax import lax
from jax.experimental import pallas as pl
from jax.experimental.pallas import tpu as pltpu
from jax.sharding import PartitionSpec as P

GRID = 16
DIRECTIONS = ((-1, -1), (-1, 0), (-1, 1), (0, -1), (0, 1), (1, -1), (1, 0), (1, 1))
STIFFNESS = 0.25
CHUNKS = 4
MESH = pl.DeviceIdType.MESH
HIGHEST = lax.Precision.HIGHEST
F32 = jnp.float32
BF16 = jnp.bfloat16


def spline(knot, frac, rows):
    cell = lax.broadcasted_iota(jnp.int32, (rows, knot.shape[1]), 0).astype(F32)
    t = (knot - cell) + frac
    s = jnp.abs(t)
    p = jnp.maximum(2.0 - s, 0.0)
    q = jnp.maximum(1.0 - s, 0.0)
    p2 = p * p
    q2 = q * q
    basis = (p2 * p) * (1.0 / 6.0) - (q2 * q) * (4.0 / 6.0)
    down = 2.0 * q2 - 0.5 * p2
    slope = jnp.where(t < 0.0, -down, down)
    return basis, slope


def kernel(
    n_row, n_col, stored,
    grids, poses, nodes, lists, first, second, live, knots, offsets,
    out,
    send_buf, ghost, pose_out, pose_in, react, ret, cube, weights, fields, lever,
    send_sem, recv_sem, psend_sem, precv_sem, rsend_sem, rrecv_sem,
):
    r = lax.axis_index("row")
    c = lax.axis_index("col")
    grains = grids.shape[0]
    capacity = lists.shape[1]
    pairs = knots.shape[0]
    count = knots.shape[1] // 3
    plane = GRID * GRID
    slots = 8 * capacity
    width = grids.shape[1] // CHUNKS

    def there(d):
        dr, dc = DIRECTIONS[d]
        rr, cc = r + dr, c + dc
        ok = (rr >= 0) & (rr < n_row) & (cc >= 0) & (cc < n_col)
        return ok, (rr, cc)

    peers = sum(there(d)[0].astype(jnp.int32) for d in range(8))
    barrier = pltpu.get_barrier_semaphore()
    for d in range(8):
        ok, place = there(d)

        @pl.when(ok)
        def _():
            pl.semaphore_signal(barrier, inc=1, device_id=place, device_id_type=MESH)

        @pl.when(jnp.logical_not(ok))
        def _():
            ghost[d * capacity:(d + 1) * capacity, :] = jnp.zeros((capacity, grids.shape[1]), BF16)
            pose_in[d] = jnp.zeros(pose_in.shape[1:], F32)
            ret[d] = jnp.zeros(ret.shape[1:], F32)

    first_row = first[...]
    sdf_row = second[...]
    live_row = live[...].astype(F32)
    stacked = jnp.concatenate(
        [first_row.astype(F32), sdf_row.astype(F32), jnp.zeros((6, pairs), F32)], axis=0).T
    first_col = stacked[:, 0:1]
    sdf_col = stacked[:, 1:2]
    spare = jnp.zeros((8, -capacity % 128), F32)
    turned = jnp.concatenate([lists[...].astype(F32), spare], axis=1).T
    send_col = jnp.concatenate([turned[:capacity, d:d + 1] for d in range(8)], axis=0)

    lane_grains = lax.broadcasted_iota(jnp.int32, (1, grains), 1).astype(F32)
    oh_send = jnp.where(send_col == lane_grains, 1.0, 0.0).astype(BF16)

    pose_out[...] = jnp.zeros(pose_out.shape, F32)
    sub_grains = lax.broadcasted_iota(jnp.int32, (grains, 1), 0)
    for d in range(8):
        picked = jnp.where(lists[d:d + 1, :] == sub_grains, 1.0, 0.0)
        pose_out[d, 0:12, 0:capacity] = jnp.dot(
            poses[...], picked, preferred_element_type=F32, precision=HIGHEST)

    def pose_copy(d):
        return pltpu.make_async_remote_copy(
            src_ref=pose_out.at[d], dst_ref=pose_in.at[7 - d],
            send_sem=psend_sem.at[d], recv_sem=precv_sem.at[7 - d],
            device_id=there(d)[1], device_id_type=MESH)

    def grid_copy(d, k):
        return pltpu.make_async_remote_copy(
            src_ref=send_buf.at[pl.ds(d * capacity, capacity), pl.ds(k * width, width)],
            dst_ref=ghost.at[pl.ds((7 - d) * capacity, capacity), pl.ds(k * width, width)],
            send_sem=send_sem.at[d, k], recv_sem=recv_sem.at[7 - d, k],
            device_id=there(d)[1], device_id_type=MESH)

    def react_copy(d):
        return pltpu.make_async_remote_copy(
            src_ref=react.at[d], dst_ref=ret.at[7 - d],
            send_sem=rsend_sem.at[d], recv_sem=rrecv_sem.at[7 - d],
            device_id=there(d)[1], device_id_type=MESH)

    order = (0, 2, 5, 7, 3, 4, 1, 6)
    for k in range(CHUNKS):
        def gather(j, carry, k=k):
            at = pl.ds(pl.multiple_of(k * width + j * plane, plane), plane)
            send_buf[:, at] = jnp.dot(
                oh_send, grids[:, at], preferred_element_type=F32).astype(BF16)
            return carry

        lax.fori_loop(0, width // plane, gather, 0, unroll=True)
        if k == 0:
            pl.semaphore_wait(barrier, peers)
        for d in order:
            @pl.when(there(d)[0])
            def _():
                grid_copy(d, k).start()
    for d in range(8):
        @pl.when(there(d)[0])
        def _():
            pose_copy(d).start()

    oh_own = jnp.where(sdf_col == lane_grains, 1.0, 0.0).astype(BF16)
    oh_first = jnp.where(first_col == lane_grains, 1.0, 0.0).astype(BF16)

    def own_cube(a, carry):
        at = pl.ds(pl.multiple_of(a * plane, plane), plane)
        found = jnp.dot(oh_own, grids[:, at], preferred_element_type=F32)
        for h in range(plane // 128):
            cube[h, pl.ds(pl.multiple_of(a * pairs, pairs), pairs), :] = found[:, h * 128:(h + 1) * 128]
        return carry

    lax.fori_loop(0, GRID, own_cube, 0, unroll=4)

    body = nodes[...]
    high = body.astype(BF16)
    low = (body - high.astype(F32)).astype(BF16)
    lever[...] = (jnp.dot(oh_first, high, preferred_element_type=F32)
                  + jnp.dot(oh_first, low, preferred_element_type=F32))

    def pair_weights(p, slot):
        knot = knots[pl.ds(p, 1), :].astype(F32)
        frac = offsets[pl.ds(p, 1), :]
        by, sy = spline(knot[:, count:2 * count], frac[:, count:2 * count], GRID)
        bz, sz = spline(knot[:, 2 * count:], frac[:, 2 * count:], GRID)
        for b in range(GRID):
            y = by[b:b + 1, :]
            weights[slot, b * GRID:(b + 1) * GRID, 0:count] = (y * bz).astype(BF16)
            weights[slot, b * GRID:(b + 1) * GRID, count:2 * count] = (
                sy[b:b + 1, :] * bz).astype(BF16)
            weights[slot, b * GRID:(b + 1) * GRID, 2 * count:] = (y * sz).astype(BF16)

    def build(p, carry):
        pair_weights(p, p)
        return carry

    lax.fori_loop(0, stored, build, 0)

    for d in range(8):
        @pl.when(there(d)[0])
        def _():
            pose_copy(d).wait_send()
            for k in range(CHUNKS):
                grid_copy(d, k).wait_send()

        back = 7 - d

        @pl.when(there(d)[0])
        def _():
            pltpu.make_async_remote_copy(
                src_ref=pose_out.at[back], dst_ref=pose_in.at[d],
                send_sem=psend_sem.at[back], recv_sem=precv_sem.at[d],
                device_id=there(d)[1], device_id_type=MESH).wait_recv()
            for k in range(CHUNKS):
                pltpu.make_async_remote_copy(
                    src_ref=send_buf.at[pl.ds(back * capacity, capacity), pl.ds(k * width, width)],
                    dst_ref=ghost.at[pl.ds(d * capacity, capacity), pl.ds(k * width, width)],
                    send_sem=send_sem.at[back, k], recv_sem=recv_sem.at[d, k],
                    device_id=there(d)[1], device_id_type=MESH).wait_recv()

    lane_slots = lax.broadcasted_iota(jnp.int32, (1, slots), 1).astype(F32)
    oh_ghost = jnp.where(sdf_col - float(grains) == lane_slots, 1.0, 0.0).astype(BF16)

    def ghost_cube(a, carry):
        at = pl.ds(pl.multiple_of(a * plane, plane), plane)
        found = jnp.dot(oh_ghost, ghost[:, at], preferred_element_type=F32)
        for h in range(plane // 128):
            cube[h, pl.ds(pl.multiple_of(a * pairs, pairs), pairs), :] += found[:, h * 128:(h + 1) * 128]
        return carry

    lax.fori_loop(0, GRID, ghost_cube, 0, unroll=4)

    def pair_fields(p, slot):
        knot = knots[pl.ds(p, 1), :].astype(F32)
        frac = offsets[pl.ds(p, 1), :]
        bx, sx = spline(knot[:, :count], frac[:, :count], GRID)
        bx = bx.astype(BF16).astype(F32)
        sx = sx.astype(BF16).astype(F32)
        at = pl.ds(p, GRID, stride=pairs)
        g = jnp.concatenate([cube[0, at, :], cube[1, at, :]], axis=1).astype(BF16)
        s = jnp.dot(g, weights[slot], preferred_element_type=F32)
        plain = s[:, :count]
        fields[0, pl.ds(p, 1), :] = jnp.sum(plain * bx, axis=0, keepdims=True)
        fields[1, pl.ds(p, 1), :] = jnp.sum(plain * sx, axis=0, keepdims=True)
        fields[2, pl.ds(p, 1), :] = jnp.sum(s[:, count:2 * count] * bx, axis=0, keepdims=True)
        fields[3, pl.ds(p, 1), :] = jnp.sum(s[:, 2 * count:] * bx, axis=0, keepdims=True)

    def contract(i, carry):
        for u in range(8):
            pair_fields(i * 8 + u, i * 8 + u)
        return carry

    lax.fori_loop(0, stored // 8, contract, 0)

    def late(i, carry):
        for u in range(4):
            pair_weights(stored + i * 4 + u, i * 4 + u)
        for u in range(4):
            pair_fields(stored + i * 4 + u, i * 4 + u)
        return carry

    if stored < pairs:
        lax.fori_loop(0, (pairs - stored) // 4, late, 0)

    push = STIFFNESS * jnp.maximum(-fields[0], 0.0)
    lane = lax.broadcasted_iota(jnp.int32, (pairs, 128), 1)
    gathered = jnp.zeros((pairs, 128), F32)
    for k in range(3):
        g = push * fields[1 + k]
        gathered = jnp.where(lane == k, jnp.sum(g, axis=1, keepdims=True), gathered)
        for i in range(3):
            moved = jnp.sum(g * lever[:, i * count:(i + 1) * count], axis=1, keepdims=True)
            gathered = jnp.where(lane == 3 + 3 * i + k, moved, gathered)
    sums = gathered.T

    own_first = jnp.where(first_row == sub_grains, 1.0, 0.0)
    own_second = jnp.where(sdf_row == sub_grains, 1.0, 0.0)
    pose1 = jnp.dot(poses[...], own_first, preferred_element_type=F32, precision=HIGHEST)
    pose2 = jnp.dot(poses[...], own_second, preferred_element_type=F32, precision=HIGHEST)
    sub_cap = lax.broadcasted_iota(jnp.int32, (capacity, 1), 0)
    for d in range(8):
        picked = jnp.where(sdf_row - (grains + d * capacity) == sub_cap, 1.0, 0.0)
        pose2 = pose2 + jnp.dot(
            pose_in[d, 0:12, 0:capacity], picked, preferred_element_type=F32, precision=HIGHEST)

    def rot(pose, i, j):
        k = 3 + 3 * i + j
        return pose[k:k + 1, :]

    total = [sums[k:k + 1, :] for k in range(3)]
    force = [sum(rot(pose2, i, j) * total[j] for j in range(3)) for i in range(3)]
    half = [[sum(sums[3 + 3 * i + j:4 + 3 * i + j, :] * rot(pose2, s, j) for j in range(3))
             for s in range(3)] for i in range(3)]
    full = [[sum(rot(pose1, q, i) * half[i][s] for i in range(3)) for s in range(3)]
            for q in range(3)]
    moment = [full[1][2] - full[2][1], full[2][0] - full[0][2], full[0][1] - full[1][0]]
    apart = [pose1[k:k + 1, :] - pose2[k:k + 1, :] for k in range(3)]
    other = [-(apart[1] * force[2] - apart[2] * force[1] + moment[0]),
             -(apart[2] * force[0] - apart[0] * force[2] + moment[1]),
             -(apart[0] * force[1] - apart[1] * force[0] + moment[2])]
    blank = jnp.zeros((2, pairs), F32)
    on_first = jnp.concatenate(force + moment + [blank], axis=0) * live_row
    on_second = jnp.concatenate([-f for f in force] + other + [blank], axis=0) * live_row

    lane_ret = lax.broadcasted_iota(jnp.int32, (1, react.shape[2]), 1).astype(F32)
    for d in range(8):
        picked = jnp.where(sdf_col - float(grains + d * capacity) == lane_ret, 1.0, 0.0)
        react[d] = jnp.dot(on_second, picked, preferred_element_type=F32, precision=HIGHEST)

        @pl.when(there(d)[0])
        def _():
            react_copy(d).start()

    loads = (jnp.dot(on_first, oh_first.astype(F32), preferred_element_type=F32, precision=HIGHEST)
             + jnp.dot(on_second, oh_own.astype(F32), preferred_element_type=F32, precision=HIGHEST))
    for d in range(8):
        back = 7 - d

        @pl.when(there(d)[0])
        def _():
            react_copy(d).wait_send()
            pltpu.make_async_remote_copy(
                src_ref=react.at[back], dst_ref=ret.at[d],
                send_sem=rsend_sem.at[back], recv_sem=rrecv_sem.at[d],
                device_id=there(d)[1], device_id_type=MESH).wait_recv()

        picked = jnp.where(send_col[d * capacity:(d + 1) * capacity, :] == lane_grains, 1.0, 0.0)
        loads = loads + jnp.dot(
            ret[d][:, 0:capacity], picked, preferred_element_type=F32, precision=HIGHEST)
    out[...] = loads[0:6, :]


def local(
    n_row, n_col,
    sdf_grids, grain_poses, surface_nodes, send_list,
    pair_first, pair_sdf, pair_pose, pair_live, knot_cells, offsets,
):
    grains, cells = sdf_grids.shape
    capacity = send_list.shape[3]
    pairs = pair_first.shape[0]
    slots = 8 * capacity
    count = knot_cells.shape[1] // 3
    stored = min(pairs, 120)
    lists = send_list.reshape(8, capacity)
    vmem = pl.BlockSpec(memory_space=pltpu.VMEM)
    return pl.pallas_call(
        functools.partial(kernel, n_row, n_col, stored),
        out_shape=jax.ShapeDtypeStruct((6, grains), F32),
        in_specs=[vmem] * 9,
        out_specs=vmem,
        scratch_shapes=[
            pltpu.VMEM((slots, cells), BF16),
            pltpu.VMEM((slots, cells), BF16),
            pltpu.VMEM((8, 16, 128), F32),
            pltpu.VMEM((8, 16, 128), F32),
            pltpu.VMEM((8, 8, 128), F32),
            pltpu.VMEM((8, 8, 128), F32),
            pltpu.VMEM((GRID * GRID // 128, pairs * GRID, 128), F32),
            pltpu.VMEM((stored, GRID * GRID, 3 * count), BF16),
            pltpu.VMEM((4, pairs, count), F32),
            pltpu.VMEM((pairs, 3 * count), F32),
            pltpu.SemaphoreType.DMA((8, CHUNKS)),
            pltpu.SemaphoreType.DMA((8, CHUNKS)),
            pltpu.SemaphoreType.DMA((8,)),
            pltpu.SemaphoreType.DMA((8,)),
            pltpu.SemaphoreType.DMA((8,)),
            pltpu.SemaphoreType.DMA((8,)),
        ],
        compiler_params=pltpu.CompilerParams(
            collective_id=0, has_side_effects=True, vmem_limit_bytes=64 * 2**20 - 65536),
    )(sdf_grids, grain_poses, surface_nodes, lists, pair_first.reshape(1, pairs),
      pair_sdf.reshape(1, pairs), pair_live.reshape(1, pairs), knot_cells, offsets)


def solution(mesh):
    in_specs = (
        P(("row", "col"), None),
        P(None, ("row", "col")),
        P(("row", "col"), None),
        P("row", "col", None, None),
        P(("row", "col")),
        P(("row", "col")),
        P(("row", "col")),
        P(("row", "col")),
        P(("row", "col"), None),
        P(("row", "col"), None),
    )
    out_specs = P(None, ("row", "col"))
    body = functools.partial(local, mesh.shape["row"], mesh.shape["col"])
    return jax.shard_map(body, mesh=mesh, in_specs=in_specs, out_specs=out_specs, check_vma=False)
```
